32 devices in a mesh: groups: 2 (over x), row: 8 (over z, y), col: 2 (over core).
Axes of the slice: x: 2, y: 2, z: 4, core: 2. Of those that a mesh axis runs over, the one named last changes fastest.
Arguments:
- queries: bfloat16 [16384, 512], P(('groups', 'row'), 'col'), parts along dimension 0, may hold values from -6 to 6
- keys: bfloat16 [16384, 512], P(('groups', 'row'), 'col'), parts along dimension 0, may hold values from -6 to 6
- values: bfloat16 [16384, 512], P(('groups', 'row'), 'col'), parts along dimension 0, may hold values from -6 to 6
- attended: bfloat16 [16384, 512], P(('groups', 'row'), 'col'), parts along dimension 0, may hold values from -6 to 6
- grad_out: bfloat16 [16384, 512], P(('groups', 'row'), 'col'), parts along dimension 0, may hold values from -2 to 2
- log_norms: bfloat16 [16384, 8], P(('groups', 'row'), 'col'), parts along dimension 0, may hold values from 2 to 4
- block_slot: int32 [64], P('groups'), parts along dimension 0, may hold values from 0 to 31, as said below
- neighbours: int32 [64, 8], P('groups'), parts along dimension 0, may hold values from 0 to 31, as said below
- live_count: int32 [64], P('groups'), parts along dimension 0, may hold values from 3 to 8
Outputs:
- query_grad: bfloat16 [16384, 512], P(('groups', 'row'), 'col'), parts along dimension 0
- key_grad: bfloat16 [16384, 512], P(('groups', 'row'), 'col'), parts along dimension 0
- value_grad: bfloat16 [16384, 512], P(('groups', 'row'), 'col'), parts along dimension 0
The draws below stay inside these ranges and needn't reach their ends.
There are 2 independent parts, one for each index of `groups`. The reference program is written for one: setup_inputs(seed, part) draws one part's arguments, and reference() takes and returns one part's arrays. A program takes and returns all parts, laid end to end along the dimension named above; each array names one. Nothing has to cross between parts.
Inputs may be any that keep to these rules, and one draw needn't show every extreme that they name: `block_slot`: a permutation: every slot holds exactly one block. `neighbours`: over the 32 list entries of the blocks held by one row index, at most 4 name blocks held by any one row index, and for every row index some row index is named by exactly 4 of them; entries at or beyond live_count carry no weight but name blocks too.
All inputs are finite; a program needn't handle non-finite values.
Results may differ from the reference program's by a relative error of at most 0.0093.
Values may be sent and summed in bfloat16 or wider, within the bound.
A program may use at most 128 MiB of HBM per device.

```python
import jax
import jax.numpy as jnp
from jax import lax

HEADS = 8
HEAD_DIM = 64
D = 512
BLOCK = 256
NEIGH = 8
BPD = 4
NB = 32
TOKENS = 8192
N_ROW = 8


def slide_layout(key):
    key_perm, key_rows, key_local = jax.random.split(key, 3)
    held = jax.random.permutation(key_perm, NB).astype(jnp.int32)
    slot_of = jnp.zeros((NB,), jnp.int32).at[held].set(jnp.arange(NB, dtype=jnp.int32))
    entries = NEIGH * BPD
    orders = jax.vmap(lambda k: jax.random.permutation(k, N_ROW))(jax.random.split(key_rows, N_ROW)).astype(jnp.int32)
    target_row = orders[:, jnp.arange(entries) % N_ROW]
    target_local = jax.random.randint(key_local, (N_ROW, entries), 0, BPD).astype(jnp.int32)
    target_slot = (target_row * BPD + target_local).reshape(NB, NEIGH)
    named = jnp.take(held, target_slot, axis=0)
    lists = jnp.zeros((NB, NEIGH), jnp.int32).at[held].set(named)
    return (slot_of, lists)


def draw_block_slot(key, part):
    return slide_layout(key)[0]


def draw_neighbours(key, part):
    return slide_layout(key)[1]


def plant(values, stream_key, least, largest):
    index_at = [jax.random.randint(jax.random.fold_in(stream_key, axis), (), 0, length) for axis, length in enumerate(values.shape)]
    widest = values.shape.index(max(values.shape))
    beside = index_at[:widest] + [(index_at[widest] + 1) % values.shape[widest]] + index_at[widest + 1:]
    return values.at[tuple(index_at)].set(least).at[tuple(beside)].set(largest)


def block_levels(stream_key, shape, cuts, low, largest):
    def one(position, parts):
        heights = jax.random.uniform(jax.random.fold_in(jax.random.fold_in(stream_key, 6), position), (parts,), jnp.float32, low / len(cuts), largest / len(cuts))
        return jnp.repeat(jnp.exp(heights), shape[position] // parts).reshape((-1,) + (1,) * (len(shape) - position - 1))

    loudness = one(*cuts[0])
    for cut in cuts[1:]:
        loudness = loudness * one(*cut)
    return loudness


def centred(stream_key, dims, width, most, pieces=(), kind=jnp.bfloat16):
    values = jax.random.normal(stream_key, dims, jnp.float32) * width
    if len(pieces) > 0:
        values = block_levels(stream_key, dims, pieces, -0.22, 0.18) * values
    return jnp.clip(values, min=-most, max=most).astype(kind)


def setup_inputs(seed: int = 0, part: int = 0) -> dict:
    seeds = jax.random.split(jax.random.key(seed), 10)
    part_keys = jax.random.split(jax.random.fold_in(seeds[9], part), 10)
    return {
        "queries": centred(part_keys[0], (TOKENS, D), 1.0, 6.0, ((0, 8), (1, 2))),
        "keys": centred(part_keys[1], (TOKENS, D), 1.0, 6.0, ((0, 8), (1, 2))),
        "values": centred(part_keys[2], (TOKENS, D), 1.0, 6.0, ((0, 8), (1, 2))),
        "attended": centred(part_keys[3], (TOKENS, D), 1.0, 6.0, ((0, 8), (1, 2))),
        "grad_out": centred(part_keys[4], (TOKENS, D), 0.3, 2.0, ((0, 8), (1, 2))),
        "log_norms": jnp.clip(2.0 + 2.0 * jax.random.uniform(part_keys[5], (TOKENS, HEADS), jnp.float32) ** block_levels(part_keys[5], (TOKENS, HEADS), ((0, 8), (1, 2)), -0.2, 0.2), 2.0, 4.0).astype(jnp.bfloat16),
        "block_slot": draw_block_slot(jax.random.fold_in(jax.random.fold_in(seeds[9], part), 71), part),
        "neighbours": draw_neighbours(jax.random.fold_in(jax.random.fold_in(seeds[9], part), 71), part),
        "live_count": plant(jax.random.randint(part_keys[8], (NB,), 3, 9), jax.random.fold_in(part_keys[8], 1), 3, 8).astype(jnp.int32),
    }


SCALE = 0.125


def lowered(array):
    return lax.optimization_barrier(array.astype(jnp.bfloat16)).astype(jnp.float32)


def reference(queries, keys, values, attended, grad_out, log_norms, block_slot, neighbours, live_count):
    tokens = queries.shape[0]
    blocks = tokens // BLOCK
    held = jnp.zeros((blocks,), jnp.int32).at[block_slot].set(jnp.arange(blocks, dtype=jnp.int32))
    target = jnp.take(block_slot, jnp.take(neighbours, held, axis=0), axis=0).astype(jnp.int32)
    weights = (jnp.arange(NEIGH, dtype=jnp.int32)[None, :] < jnp.take(live_count, held)[:, None]).astype(jnp.float32)

    def split(array):
        return array.reshape(blocks, BLOCK, HEADS, HEAD_DIM)

    query_h = split(queries)
    key_h = split(keys)
    value_h = split(values)
    out_h = split(attended)
    grad_h = split(grad_out)
    delta = jnp.sum(grad_h.astype(jnp.float32) * out_h.astype(jnp.float32), axis=3).astype(jnp.bfloat16)
    norms = log_norms.reshape(blocks, BLOCK, HEADS)

    def step(carry, index):
        key_acc, value_acc = carry
        rows = target[index]
        key_part = jnp.take(key_h, rows, axis=0).astype(jnp.float32)
        value_part = jnp.take(value_h, rows, axis=0).astype(jnp.float32)
        query_f = query_h[index].astype(jnp.float32)
        grad_f = grad_h[index].astype(jnp.float32)
        shift = jnp.transpose(norms[index].astype(jnp.float32))[None, :, :, None]
        offset = jnp.transpose(delta[index].astype(jnp.float32))[None, :, :, None]
        scores = jnp.einsum('qhe,jkhe->jhqk', query_f, key_part) * SCALE
        prob = jnp.exp(scores - shift) * weights[index][:, None, None, None]
        prob_low = lowered(prob)
        dprob = jnp.einsum('qhe,jkhe->jhqk', grad_f, value_part)
        dscore = lowered(prob * (dprob - offset))
        query_part = lowered(jnp.einsum('jhqk,jkhe->jqhe', dscore, key_part) * SCALE)
        key_grad = lowered(jnp.einsum('jhqk,qhe->jkhe', dscore, query_f) * SCALE)
        value_grad = lowered(jnp.einsum('jhqk,qhe->jkhe', prob_low, grad_f))
        key_acc = key_acc.at[rows].add(key_grad)
        value_acc = value_acc.at[rows].add(value_grad)
        return (key_acc, value_acc), jnp.sum(query_part, axis=0)

    zeros = jnp.zeros((blocks, BLOCK, HEADS, HEAD_DIM), jnp.float32)
    (key_acc, value_acc), query_grad = lax.scan(step, (zeros, zeros), jnp.arange(blocks, dtype=jnp.int32))
    shape = (tokens, HEADS * HEAD_DIM)
    return (query_grad.reshape(shape).astype(jnp.bfloat16),
            key_acc.reshape(shape).astype(jnp.bfloat16),
            value_acc.reshape(shape).astype(jnp.bfloat16))
```

```python
import functools

import jax
import jax.numpy as jnp
from jax import lax
from jax.experimental import pallas as pl
from jax.experimental.pallas import tpu as pltpu
from jax.sharding import PartitionSpec as P

BLOCK = 256
NEIGH = 8
SCALE = 0.125
HEAD = 64
PAIR = 2 * HEAD
STATS = 16


def nt(a, b):
    return lax.dot_general(a, b, (((1,), (1,)), ((), ())), preferred_element_type=jnp.float32)


def nn(a, b):
    return lax.dot_general(a, b, (((1,), (0,)), ((), ())), preferred_element_type=jnp.float32)


def grads_kernel(
    here_ref, slot_ref, near_ref, live_ref, load_ref, key_ref, value_ref,
    dq_ref, dk_ref, dv_ref,
    src_list, dst_list, dq_acc, dk_acc, dv_acc, key_m, value_m, key_t,
):
    blocks = slot_ref.shape[0]
    per_row = key_ref.shape[0]
    first = here_ref[0] * per_row

    def scan_block(b, count):
        source = slot_ref[b]
        live = live_ref[b]

        def scan_entry(j, count):
            target = slot_ref[near_ref[b * NEIGH + j]] - first
            mine = (target >= 0) & (target < per_row) & (j < live)

            @pl.when(mine)
            def _():
                src_list[count] = source
                dst_list[count] = target

            return count + mine.astype(jnp.int32)

        return lax.fori_loop(0, NEIGH, scan_entry, count, unroll=True)

    count = lax.fori_loop(0, blocks, scan_block, jnp.int32(0))

    dk_acc[...] = jnp.zeros_like(dk_acc)
    dv_acc[...] = jnp.zeros_like(dv_acc)

    @pl.loop(0, blocks)
    def _(s):
        dq_acc[s] = jnp.zeros(dq_acc.shape[1:], jnp.float32)

    low = lax.broadcasted_iota(jnp.int32, (BLOCK, PAIR), 1) < HEAD
    for t in range(per_row):
        key = key_ref[t].astype(jnp.float32) * SCALE
        value = value_ref[t].astype(jnp.float32)
        for h in range(2):
            mask = low if h == 0 else ~low
            masked = jnp.where(mask, key, 0.0)
            key_m[t, h * BLOCK:(h + 1) * BLOCK] = masked.astype(jnp.bfloat16)
            value_m[t, h * BLOCK:(h + 1) * BLOCK] = jnp.where(mask, value, 0.0).astype(jnp.bfloat16)
            key_t[t, :, h * BLOCK:(h + 1) * BLOCK] = masked.T.astype(jnp.bfloat16)

    @pl.loop(0, count)
    def _(e):
        s = src_list[e]
        t = dst_list[e]
        query = load_ref[s, 0:BLOCK]
        grad = load_ref[s, BLOCK:2 * BLOCK]
        stats = load_ref[s, 2 * BLOCK:2 * BLOCK + STATS].astype(jnp.float32)

        def row(i):
            return jnp.concatenate([stats[2 * i:2 * i + 1], stats[2 * i + 1:2 * i + 2]], axis=1)

        score = nt(key_m[t], query)
        dprob = nt(value_m[t], grad)
        probs, dscores = [], []
        for h in range(2):
            part = slice(h * BLOCK, (h + 1) * BLOCK)
            prob = jnp.exp(score[part] - row(h))
            dscores.append((prob * (dprob[part] - row(2 + h))).astype(jnp.bfloat16))
            probs.append(prob.astype(jnp.bfloat16))
        dv_acc[t] += jnp.where(low, nn(probs[0], grad), nn(probs[1], grad))
        dk_acc[t] += jnp.where(low, nn(dscores[0], query), nn(dscores[1], query))
        dq_acc[s] += nn(key_t[t], jnp.concatenate(dscores, axis=0))

    dk_ref[...] = (dk_acc[...] * SCALE).astype(jnp.bfloat16)
    dv_ref[...] = dv_acc[...].astype(jnp.bfloat16)

    @pl.loop(0, blocks)
    def _(s):
        dq_ref[s] = dq_acc[s].astype(jnp.bfloat16)


def local_grads(here, slots, near, live, load, key, value):
    blocks, rows, _ = load.shape
    per_row = key.shape[0]
    smem = pl.BlockSpec(memory_space=pltpu.SMEM)
    vmem = pl.BlockSpec(memory_space=pltpu.VMEM)
    most = per_row * NEIGH * 4
    return pl.pallas_call(
        grads_kernel,
        out_shape=(
            jax.ShapeDtypeStruct((blocks, PAIR, BLOCK), jnp.bfloat16),
            jax.ShapeDtypeStruct(key.shape, jnp.bfloat16),
            jax.ShapeDtypeStruct(key.shape, jnp.bfloat16),
        ),
        in_specs=[smem] * 4 + [vmem] * 3,
        out_specs=(vmem, vmem, vmem),
        scratch_shapes=[
            pltpu.SMEM((most,), jnp.int32),
            pltpu.SMEM((most,), jnp.int32),
            pltpu.VMEM((blocks, PAIR, BLOCK), jnp.float32),
            pltpu.VMEM(key.shape, jnp.float32),
            pltpu.VMEM(key.shape, jnp.float32),
            pltpu.VMEM((per_row, 2 * BLOCK, PAIR), jnp.bfloat16),
            pltpu.VMEM((per_row, 2 * BLOCK, PAIR), jnp.bfloat16),
            pltpu.VMEM((per_row, PAIR, 2 * BLOCK), jnp.bfloat16),
        ],
        compiler_params=pltpu.CompilerParams(vmem_limit_bytes=56 * 2**20),
        cost_estimate=pl.CostEstimate(
            flops=10 * 32 * 2 * BLOCK * BLOCK * PAIR, bytes_accessed=8 * 2**20, transcendentals=0
        ),
    )(here, slots, near, live, load, key, value)


def body(queries, keys, values, attended, grad_out, log_norms, block_slot, neighbours, live_count):
    here = lax.axis_index("row").astype(jnp.int32).reshape(1)
    tokens, width = queries.shape
    per_row = tokens // BLOCK
    heads = log_norms.shape[1]
    near = neighbours.reshape(-1)
    delta = jnp.sum(
        (grad_out.astype(jnp.float32) * attended.astype(jnp.float32)).reshape(tokens, heads, HEAD),
        axis=2,
    ).astype(jnp.bfloat16)
    loads = []
    for c in range(heads // 2):
        lanes = slice(c * PAIR, (c + 1) * PAIR)
        stats = jnp.concatenate([log_norms[:, 2 * c:2 * c + 2], delta[:, 2 * c:2 * c + 2]], axis=1)
        stats = jnp.transpose(stats.reshape(per_row, BLOCK, 4), (0, 2, 1)).reshape(per_row, 8, PAIR)
        loads.append(jnp.concatenate([
            queries[:, lanes].reshape(per_row, BLOCK, PAIR),
            grad_out[:, lanes].reshape(per_row, BLOCK, PAIR),
            stats,
            jnp.zeros((per_row, STATS - 8, PAIR), jnp.bfloat16),
        ], axis=1))
    everyone = [lax.all_gather(load, "row", axis=0, tiled=True) for load in loads]
    dqs, dks, dvs = [], [], []
    for c in range(heads // 2):
        lanes = slice(c * PAIR, (c + 1) * PAIR)
        dq, dk, dv = local_grads(
            here, block_slot, near, live_count, everyone[c],
            keys[:, lanes].reshape(per_row, BLOCK, PAIR),
            values[:, lanes].reshape(per_row, BLOCK, PAIR),
        )
        dq = lax.psum_scatter(dq, "row", scatter_dimension=0, tiled=True)
        dqs.append(jnp.transpose(dq, (0, 2, 1)).reshape(tokens, PAIR))
        dks.append(dk.reshape(tokens, PAIR))
        dvs.append(dv.reshape(tokens, PAIR))
    return tuple(jnp.concatenate(x, axis=1) for x in (dqs, dks, dvs))


def solution(mesh):
    tokens = P(("groups", "row"), "col")
    return jax.shard_map(
        body,
        mesh=mesh,
        in_specs=(tokens,) * 6 + (P("groups"), P("groups", None), P("groups")),
        out_specs=(tokens,) * 3,
        check_vma=False,
    )
```

```python
import functools

import jax
import jax.numpy as jnp
from jax import lax
from jax.experimental import pallas as pl
from jax.experimental.pallas import tpu as pltpu
from jax.sharding import PartitionSpec as P

BLOCK = 256
NEIGH = 8
SCALE = 0.125
HEAD = 64
PAIR = 2 * HEAD
STATS = 16


def nt(a, b):
    return lax.dot_general(a, b, (((1,), (1,)), ((), ())), preferred_element_type=jnp.float32)


def nn(a, b):
    return lax.dot_general(a, b, (((1,), (0,)), ((), ())), preferred_element_type=jnp.float32)


def scan_kernel(here_ref, slot_ref, near_ref, live_ref, count_ref, entry_ref):
    blocks = slot_ref.shape[0]
    n_row = count_ref.shape[0]
    per_row = blocks // n_row
    first = here_ref[0] * per_row
    room = NEIGH * per_row

    @pl.loop(0, n_row)
    def _(r):
        count_ref[r] = 0

    @pl.loop(0, blocks)
    def _(b):
        source = slot_ref[b]
        row = source // per_row
        live = live_ref[b]

        def scan_entry(j, count):
            target = slot_ref[near_ref[b * NEIGH + j]] - first
            mine = (target >= 0) & (target < per_row) & (j < live)

            @pl.when(mine)
            def _():
                entry_ref[row * room + count] = (source - row * per_row) * per_row + target

            return count + mine.astype(jnp.int32)

        count_ref[row] = lax.fori_loop(0, NEIGH, scan_entry, count_ref[row], unroll=True)


def scan_lists(here, slots, near, live, n_row):
    smem = pl.BlockSpec(memory_space=pltpu.SMEM)
    return pl.pallas_call(
        scan_kernel,
        out_shape=(
            jax.ShapeDtypeStruct((n_row,), jnp.int32),
            jax.ShapeDtypeStruct((slots.shape[0] * NEIGH,), jnp.int32),
        ),
        in_specs=[smem] * 4,
        out_specs=(smem, smem),
    )(here, slots, near, live)


def grads_kernel(n_load, first, row_ref, count_ref, entry_ref, key_ref, value_ref, *refs):
    loads, refs = refs[:n_load], refs[n_load:]
    if not first:
        dk_old, dv_old = refs[:2]
        refs = refs[2:]
    dqs, refs = refs[:n_load], refs[n_load:]
    dk_acc, dv_acc, dq_acc, key_m, value_m, key_t = refs
    per_row = key_ref.shape[0]
    pairs = key_ref.shape[2] // PAIR
    room = NEIGH * per_row
    if first:
        dk_acc[...] = jnp.zeros_like(dk_acc)
        dv_acc[...] = jnp.zeros_like(dv_acc)
    else:
        dk_acc[...] = dk_old[...]
        dv_acc[...] = dv_old[...]

    low = lax.broadcasted_iota(jnp.int32, (BLOCK, PAIR), 1) < HEAD
    for c in range(pairs):
        lanes = slice(c * PAIR, (c + 1) * PAIR)

        @pl.loop(0, per_row)
        def _(t):
            key = key_ref[t, :, lanes].astype(jnp.float32) * SCALE
            value = value_ref[t, :, lanes].astype(jnp.float32)
            for h in range(2):
                mask = low if h == 0 else ~low
                part = slice(h * BLOCK, (h + 1) * BLOCK)
                masked = jnp.where(mask, key, 0.0)
                key_m[c, t, part] = masked.astype(jnp.bfloat16)
                value_m[c, t, part] = jnp.where(mask, value, 0.0).astype(jnp.bfloat16)
                key_t[c, t, :, part] = masked.T.astype(jnp.bfloat16)

    for load_ref, dq_ref, i in zip(loads, dqs, range(n_load)):
        source_row = row_ref[i]
        dq_acc[...] = jnp.zeros_like(dq_acc)

        @pl.when(source_row >= 0)
        def _():
            @pl.loop(0, count_ref[source_row])
            def _(e):
                entry = entry_ref[source_row * room + e]
                s = entry // per_row
                t = entry % per_row
                for c in range(pairs):
                    lanes = slice(c * PAIR, (c + 1) * PAIR)
                    query = load_ref[s, 0:BLOCK, lanes]
                    grad = load_ref[s, BLOCK:2 * BLOCK, lanes]
                    stats = load_ref[s, 2 * BLOCK:2 * BLOCK + STATS].astype(jnp.float32)
                    score = nt(key_m[c, t], query)
                    dprob = nt(value_m[c, t], grad)
                    probs, dscores = [], []
                    for h in range(2):
                        part = slice(h * BLOCK, (h + 1) * BLOCK)
                        i_h = 2 * c + h
                        norm = stats[i_h:i_h + 1]
                        delta = stats[2 * pairs + i_h:2 * pairs + i_h + 1]
                        prob = jnp.exp(score[part] - norm)
                        dscores.append((prob * (dprob[part] - delta)).astype(jnp.bfloat16))
                        probs.append(prob.astype(jnp.bfloat16))
                    dv_acc[t, :, lanes] += jnp.where(low, nn(probs[0], grad), nn(probs[1], grad))
                    dk_acc[t, :, lanes] += jnp.where(low, nn(dscores[0], query), nn(dscores[1], query))
                    dq_acc[s, lanes] += nn(key_t[c, t], jnp.concatenate(dscores, axis=0))

        dq_ref[...] = dq_acc[...].astype(jnp.bfloat16)


def stage_grads(rows, counts, entries, key, value, loads, carry):
    per_row, _, width = key.shape
    pairs = width // PAIR
    n_load = len(loads)
    smem = pl.BlockSpec(memory_space=pltpu.SMEM)
    vmem = pl.BlockSpec(memory_space=pltpu.VMEM)
    part = jax.ShapeDtypeStruct((per_row, width, BLOCK), jnp.bfloat16)
    total = jax.ShapeDtypeStruct(key.shape, jnp.float32)
    outs = pl.pallas_call(
        functools.partial(grads_kernel, n_load, not carry),
        out_shape=(part,) * n_load + (total, total),
        in_specs=[smem] * 3 + [vmem] * (2 + n_load + len(carry)),
        out_specs=(vmem,) * (n_load + 2),
        scratch_shapes=[
            pltpu.VMEM((per_row, width, BLOCK), jnp.float32),
            pltpu.VMEM((pairs, per_row, 2 * BLOCK, PAIR), jnp.bfloat16),
            pltpu.VMEM((pairs, per_row, 2 * BLOCK, PAIR), jnp.bfloat16),
            pltpu.VMEM((pairs, per_row, PAIR, 2 * BLOCK), jnp.bfloat16),
        ],
        compiler_params=pltpu.CompilerParams(vmem_limit_bytes=40 * 2**20),
        cost_estimate=pl.CostEstimate(
            flops=n_load * 3000000000, bytes_accessed=n_load * 2**21, transcendentals=0
        ),
    )(rows, counts, entries, key, value, *loads, *carry)
    return outs[:n_load], outs[n_load:]


def body(queries, keys, values, attended, grad_out, log_norms, block_slot, neighbours, live_count):
    n_row = lax.axis_size("row")
    here = lax.axis_index("row").astype(jnp.int32)
    n_z = n_row // 2
    z, y = here // 2, here % 2
    tokens, width = queries.shape
    per_row = tokens // BLOCK
    heads = log_norms.shape[1]

    def swap(x, low, high):
        pairs = [(2 * k + j, 2 * k + 1 - j) for k in range(low, high) for j in range(2)]
        return lax.ppermute(x, "row", pairs)

    def shift(x, by, low, high):
        pairs = [(2 * k + j, 2 * (k + by) + j) for k in range(low, high) for j in range(2)]
        return lax.ppermute(x, "row", pairs)

    delta = jnp.sum(
        (grad_out.astype(jnp.float32) * attended.astype(jnp.float32)).reshape(tokens, heads, HEAD),
        axis=2,
    ).astype(jnp.bfloat16)
    stats = jnp.concatenate([log_norms, delta], axis=1).reshape(per_row, BLOCK, 2 * heads)
    own = jnp.concatenate([
        queries.reshape(per_row, BLOCK, width),
        grad_out.reshape(per_row, BLOCK, width),
        jnp.transpose(stats, (0, 2, 1)),
        jnp.zeros((per_row, STATS - 2 * heads, width), jnp.bfloat16),
    ], axis=1)
    key = keys.reshape(per_row, BLOCK, width)
    value = values.reshape(per_row, BLOCK, width)

    ups, downs, y_ups, y_downs = [own], [own], [swap(own, 0, n_z)], [None]
    for k in range(1, n_z):
        ups.append(shift(ups[-1], 1, k - 1, n_z - 1))
        downs.append(shift(downs[-1], -1, 1, n_z - k + 1))
        y_ups.append(swap(ups[k], k, n_z))
        y_downs.append(swap(downs[k], 0, n_z - k))

    counts, entries = scan_lists(
        here.reshape(1), block_slot, neighbours.reshape(-1), live_count, n_row
    )

    def named(kind, k):
        up = kind in ("up", "y_up")
        there = z - k if up else z + k
        side = 1 - y if kind in ("y_up", "y_down") else y
        valid = (there >= 0) & (there < n_z)
        return jnp.where(valid, 2 * there + side, -1)

    have = {"up": ups, "down": downs, "y_up": y_ups, "y_down": y_downs}
    stages = [[("up", 0), ("y_up", 0)]]
    for k in range(1, n_z + 1):
        stage = [("up", k), ("down", k)] if k < n_z else []
        stages.append(stage + ([("y_up", k - 1), ("y_down", k - 1)] if k > 1 else []))
    parts, carry = {}, ()
    for stage in stages:
        rows = jnp.stack([named(*name) for name in stage]).astype(jnp.int32)
        dqs, carry = stage_grads(
            rows, counts, entries, key, value, [have[kind][k] for kind, k in stage], carry
        )
        parts.update(zip(stage, dqs))

    def add(*terms):
        return sum(x.astype(jnp.float32) for x in terms)

    low = jnp.bfloat16
    up, down = None, None
    for k in range(n_z - 1, 0, -1):
        up_terms = [parts[("up", k)], swap(parts[("y_up", k)], k, n_z)]
        down_terms = [parts[("down", k)], swap(parts[("y_down", k)], 0, n_z - k)]
        if up is not None:
            up_terms.append(up)
            down_terms.append(down)
        up = shift(add(*up_terms).astype(low), -1, k, n_z)
        down = shift(add(*down_terms).astype(low), 1, 0, n_z - k)
    dq = add(parts[("up", 0)], swap(parts[("y_up", 0)], 0, n_z), up, down).astype(low)
    dk, dv = carry
    return (
        jnp.transpose(dq, (0, 2, 1)).reshape(tokens, width),
        (dk * SCALE).astype(low).reshape(tokens, width),
        dv.astype(low).reshape(tokens, width),
    )


def solution(mesh):
    tokens = P(("groups", "row"), "col")
    return jax.shard_map(
        body,
        mesh=mesh,
        in_specs=(tokens,) * 6 + (P("groups"), P("groups", None), P("groups")),
        out_specs=(tokens,) * 3,
        check_vma=False,
    )
```

```python
import functools

import jax
import jax.numpy as jnp
from jax import lax
from jax.experimental import pallas as pl
from jax.experimental.pallas import tpu as pltpu
from jax.sharding import PartitionSpec as P

BLOCK = 256
NEIGH = 8
SCALE = 0.125
HEAD = 64
PAIR = 2 * HEAD
STATS = 16


def nt(a, b):
    return lax.dot_general(a, b, (((1,), (1,)), ((), ())), preferred_element_type=jnp.float32)


def nn(a, b):
    return lax.dot_general(a, b, (((1,), (0,)), ((), ())), preferred_element_type=jnp.float32)


def scan_kernel(here_ref, slot_ref, near_ref, live_ref, count_ref, entry_ref):
    blocks = slot_ref.shape[0]
    n_row = count_ref.shape[0]
    per_row = blocks // n_row
    first = here_ref[0] * per_row
    room = NEIGH * per_row

    @pl.loop(0, n_row)
    def _(r):
        count_ref[r] = 0

    @pl.loop(0, blocks)
    def _(b):
        source = slot_ref[b]
        row = source // per_row
        live = live_ref[b]

        def scan_entry(j, count):
            target = slot_ref[near_ref[b * NEIGH + j]] - first
            mine = (target >= 0) & (target < per_row) & (j < live)

            @pl.when(mine)
            def _():
                entry_ref[row * room + count] = (source - row * per_row) * per_row + target

            return count + mine.astype(jnp.int32)

        count_ref[row] = lax.fori_loop(0, NEIGH, scan_entry, count_ref[row], unroll=True)


def scan_lists(here, slots, near, live, n_row):
    smem = pl.BlockSpec(memory_space=pltpu.SMEM)
    return pl.pallas_call(
        scan_kernel,
        out_shape=(
            jax.ShapeDtypeStruct((n_row,), jnp.int32),
            jax.ShapeDtypeStruct((slots.shape[0] * NEIGH,), jnp.int32),
        ),
        in_specs=[smem] * 4,
        out_specs=(smem, smem),
    )(here, slots, near, live)


def grads_kernel(offsets, first, row_ref, count_ref, entry_ref, key_ref, value_ref, *refs):
    n_load = len(offsets)
    loads, refs = refs[:n_load], refs[n_load:]
    if not first:
        dk_old, dv_old = refs[:2]
        refs = refs[2:]
    dqs, refs = refs[:n_load], refs[n_load:]
    dk_acc, dv_acc, dq_acc, key_m, value_m, key_t = refs
    per_row = key_ref.shape[0]
    pairs = key_ref.shape[2] // PAIR
    room = NEIGH * per_row
    if first:
        dk_acc[...] = jnp.zeros_like(dk_acc)
        dv_acc[...] = jnp.zeros_like(dv_acc)
    else:
        dk_acc[...] = dk_old[...]
        dv_acc[...] = dv_old[...]

    low = lax.broadcasted_iota(jnp.int32, (BLOCK, PAIR), 1) < HEAD
    for c in range(pairs):
        lanes = slice(c * PAIR, (c + 1) * PAIR)

        @pl.loop(0, per_row)
        def _(t):
            key = key_ref[t, :, lanes].astype(jnp.float32) * SCALE
            value = value_ref[t, :, lanes].astype(jnp.float32)
            for h in range(2):
                mask = low if h == 0 else ~low
                part = slice(h * BLOCK, (h + 1) * BLOCK)
                masked = jnp.where(mask, key, 0.0)
                key_m[c, t, part] = masked.astype(jnp.bfloat16)
                value_m[c, t, part] = jnp.where(mask, value, 0.0).astype(jnp.bfloat16)
                key_t[c, t, :, part] = masked.T.astype(jnp.bfloat16)

    for i, (load_ref, dq_ref, offset) in enumerate(zip(loads, dqs, offsets)):
        source_row = row_ref[i]
        held = load_ref.shape[0]
        dq_acc[0:held] = jnp.zeros((held,) + dq_acc.shape[1:], jnp.float32)

        def add_entry(s, t, load_ref=load_ref):
            for c in range(pairs):
                lanes = slice(c * PAIR, (c + 1) * PAIR)
                query = load_ref[s, 0:BLOCK, lanes]
                grad = load_ref[s, BLOCK:2 * BLOCK, lanes]
                stats = load_ref[s, 2 * BLOCK:2 * BLOCK + STATS].astype(jnp.float32)
                score = nt(key_m[c, t], query)
                dprob = nt(value_m[c, t], grad)
                probs, dscores = [], []
                for h in range(2):
                    part = slice(h * BLOCK, (h + 1) * BLOCK)
                    i_h = 2 * c + h
                    norm = stats[i_h:i_h + 1]
                    delta = stats[2 * pairs + i_h:2 * pairs + i_h + 1]
                    prob = jnp.exp(score[part] - norm)
                    dscores.append((prob * (dprob[part] - delta)).astype(jnp.bfloat16))
                    probs.append(prob.astype(jnp.bfloat16))
                dv_acc[t, :, lanes] += jnp.where(low, nn(probs[0], grad), nn(probs[1], grad))
                dk_acc[t, :, lanes] += jnp.where(low, nn(dscores[0], query), nn(dscores[1], query))
                dq_acc[s, lanes] += nn(key_t[c, t], jnp.concatenate(dscores, axis=0))

        @pl.when(source_row >= 0)
        def _():
            @pl.loop(0, count_ref[source_row])
            def _(e):
                entry = entry_ref[source_row * room + e]
                s = entry // per_row - offset
                t = entry % per_row
                if held == per_row:
                    add_entry(s, t)
                else:
                    pl.when((s >= 0) & (s < held))(lambda: add_entry(s, t))

        dq_ref[...] = dq_acc[0:held].astype(jnp.bfloat16)


def stage_grads(rows, counts, entries, key, value, loads, offsets, carry):
    per_row, _, width = key.shape
    pairs = width // PAIR
    n_load = len(loads)
    smem = pl.BlockSpec(memory_space=pltpu.SMEM)
    vmem = pl.BlockSpec(memory_space=pltpu.VMEM)
    parts = tuple(
        jax.ShapeDtypeStruct((load.shape[0], width, BLOCK), jnp.bfloat16) for load in loads
    )
    total = jax.ShapeDtypeStruct(key.shape, jnp.float32)
    outs = pl.pallas_call(
        functools.partial(grads_kernel, offsets, not carry),
        out_shape=parts + (total, total),
        in_specs=[smem] * 3 + [vmem] * (2 + n_load + len(carry)),
        out_specs=(vmem,) * (n_load + 2),
        scratch_shapes=[
            pltpu.VMEM((per_row, width, BLOCK), jnp.float32),
            pltpu.VMEM((pairs, per_row, 2 * BLOCK, PAIR), jnp.bfloat16),
            pltpu.VMEM((pairs, per_row, 2 * BLOCK, PAIR), jnp.bfloat16),
            pltpu.VMEM((pairs, per_row, PAIR, 2 * BLOCK), jnp.bfloat16),
        ],
        compiler_params=pltpu.CompilerParams(vmem_limit_bytes=40 * 2**20),
        cost_estimate=pl.CostEstimate(
            flops=n_load * 3000000000, bytes_accessed=n_load * 2**21, transcendentals=0
        ),
    )(rows, counts, entries, key, value, *loads, *carry)
    return outs[:n_load], outs[n_load:]


def body(queries, keys, values, attended, grad_out, log_norms, block_slot, neighbours, live_count):
    n_row = lax.axis_size("row")
    here = lax.axis_index("row").astype(jnp.int32)
    n_z = n_row // 2
    z, y = here // 2, here % 2
    tokens, width = queries.shape
    per_row = tokens // BLOCK
    heads = log_norms.shape[1]

    def swap(x, low, high):
        pairs = [(2 * k + j, 2 * k + 1 - j) for k in range(low, high) for j in range(2)]
        return lax.ppermute(x, "row", pairs)

    def shift(x, by, low, high):
        pairs = [(2 * k + j, 2 * (k + by) + j) for k in range(low, high) for j in range(2)]
        return lax.ppermute(x, "row", pairs)

    delta = jnp.sum(
        (grad_out.astype(jnp.float32) * attended.astype(jnp.float32)).reshape(tokens, heads, HEAD),
        axis=2,
    ).astype(jnp.bfloat16)
    stats = jnp.concatenate([log_norms, delta], axis=1).reshape(per_row, BLOCK, 2 * heads)
    own = jnp.concatenate([
        queries.reshape(per_row, BLOCK, width),
        grad_out.reshape(per_row, BLOCK, width),
        jnp.transpose(stats, (0, 2, 1)),
        jnp.zeros((per_row, STATS - 2 * heads, width), jnp.bfloat16),
    ], axis=1)
    key = keys.reshape(per_row, BLOCK, width)
    value = values.reshape(per_row, BLOCK, width)

    last = n_z - 1
    half = per_row // 2
    edge = [(j, 2 + j) for j in range(2)] + [(2 * last + j, 2 * last - 2 + j) for j in range(2)]
    have = {("up", 0): own, ("y", 0): swap(own, 0, n_z)}
    ups, downs = own, own
    for k in range(1, n_z):
        ups = shift(ups, 1, k - 1, last)
        downs = shift(downs, -1, 1, n_z - k + 1)
        have[("up", k)], have[("down", k)] = ups, downs
        if k == 1:
            have[("y_up", 1)] = swap(ups, 2, n_z)
            have[("y_down", 1)] = swap(downs, 0, n_z - 2)
            have[("y_edge", 1)] = lax.ppermute(have[("y", 0)], "row", edge)
        elif k < last:
            have[("y_up", k)] = swap(ups, k, n_z)
            have[("y_down", k)] = swap(downs, 0, n_z - k)
        else:
            have[("y_up_a", k)] = swap(ups[:half], last, n_z)
            have[("y_down_a", k)] = swap(downs[:half], 0, 1)
            have[("y_up_b", k)] = shift(have[("y_up", k - 1)][half:], 1, last - 1, last)
            have[("y_down_b", k)] = shift(have[("y_down", k - 1)][half:], -1, 1, 2)

    counts, entries = scan_lists(
        here.reshape(1), block_slot, neighbours.reshape(-1), live_count, n_row
    )

    def named(kind, k):
        if kind == "y_edge":
            there = jnp.where(z == 1, 0, jnp.where(z == last - 1, last, -1))
        else:
            there = z + k if "down" in kind else z - k
            if (kind, k) == ("y_up", 1):
                there = jnp.where(there >= 1, there, -1)
            if (kind, k) == ("y_down", 1):
                there = jnp.where(there <= last - 1, there, -1)
        side = 1 - y if kind.startswith("y") else y
        return jnp.where((there >= 0) & (there < n_z), 2 * there + side, -1)

    stages = [[("up", 0), ("y", 0)], [("up", 1), ("down", 1)]]
    stages.append([("up", 2), ("down", 2), ("y_up", 1), ("y_down", 1), ("y_edge", 1)])
    for k in range(3, n_z):
        stages.append([("up", k), ("down", k), ("y_up", k - 1), ("y_down", k - 1)])
    stages.append([(kind, last) for kind in ("y_up_a", "y_down_a", "y_up_b", "y_down_b")])
    parts, carry = {}, ()
    for stage in stages:
        rows = jnp.stack([named(*name) for name in stage]).astype(jnp.int32)
        offsets = tuple(half if name[0].endswith("_b") else 0 for name in stage)
        dqs, carry = stage_grads(
            rows, counts, entries, key, value, [have[name] for name in stage], offsets, carry
        )
        parts.update(zip(stage, dqs))

    low = jnp.bfloat16

    def add(*terms):
        return sum(x.astype(jnp.float32) for x in terms)

    def add_half(x, part, lead):
        pads = ((0, per_row - half), (0, 0), (0, 0)) if lead else ((half, 0), (0, 0), (0, 0))
        return add(x, jnp.pad(part, pads)).astype(low)

    edge_back = lax.ppermute(parts[("y_edge", 1)], "row", [(j, i) for i, j in edge])
    up_b = shift(parts[("y_up_b", last)], -1, last, n_z)
    down_b = shift(parts[("y_down_b", last)], 1, 0, 1)
    up = add_half(parts[("up", last)], swap(parts[("y_up_a", last)], last, n_z), True)
    down = add_half(parts[("down", last)], swap(parts[("y_down_a", last)], 0, 1), True)
    for k in range(last - 1, 0, -1):
        up, down = shift(up, -1, k + 1, n_z), shift(down, 1, 0, n_z - k - 1)
        y_up, y_down = parts[("y_up", k)], parts[("y_down", k)]
        if k == last - 1:
            y_up, y_down = add_half(y_up, up_b, False), add_half(y_down, down_b, False)
        edged = k == 1
        y_up = swap(y_up, 2 if edged else k, n_z)
        y_down = swap(y_down, 0, n_z - 2 if edged else n_z - k)
        up = add(parts[("up", k)], y_up, up).astype(low)
        down = add(parts[("down", k)], y_down, down).astype(low)
    up, down = shift(up, -1, 1, n_z), shift(down, 1, 0, last)
    y_back = swap(add(parts[("y", 0)], edge_back).astype(low), 0, n_z)
    dq = add(parts[("up", 0)], y_back, up, down).astype(low)
    dk, dv = carry
    return (
        jnp.transpose(dq, (0, 2, 1)).reshape(tokens, width),
        (dk * SCALE).astype(low).reshape(tokens, width),
        dv.astype(low).reshape(tokens, width),
    )


def solution(mesh):
    tokens = P(("groups", "row"), "col")
    return jax.shard_map(
        body,
        mesh=mesh,
        in_specs=(tokens,) * 6 + (P("groups"), P("groups", None), P("groups")),
        out_specs=(tokens,) * 3,
        check_vma=False,
    )
```

```python
import functools

import jax
import jax.numpy as jnp
from jax import lax
from jax.experimental import pallas as pl
from jax.experimental.pallas import tpu as pltpu
from jax.sharding import PartitionSpec as P

BLOCK = 256
NEIGH = 8
SCALE = 0.125
HEAD = 64
PAIR = 2 * HEAD
STATS = 16


def nt(a, b):
    return lax.dot_general(a, b, (((1,), (1,)), ((), ())), preferred_element_type=jnp.float32)


def nn(a, b):
    return lax.dot_general(a, b, (((1,), (0,)), ((), ())), preferred_element_type=jnp.float32)


def scan_kernel(here_ref, slot_ref, near_ref, live_ref, count_ref, entry_ref):
    blocks = slot_ref.shape[0]
    n_row = count_ref.shape[0]
    per_row = blocks // n_row
    first = here_ref[0] * per_row
    room = NEIGH * per_row

    @pl.loop(0, n_row)
    def _(r):
        count_ref[r] = 0

    @pl.loop(0, blocks)
    def _(b):
        source = slot_ref[b]
        row = source // per_row
        live = live_ref[b]

        def scan_entry(j, count):
            target = slot_ref[near_ref[b * NEIGH + j]] - first
            mine = (target >= 0) & (target < per_row) & (j < live)

            @pl.when(mine)
            def _():
                entry_ref[row * room + count] = (source - row * per_row) * per_row + target

            return count + mine.astype(jnp.int32)

        count_ref[row] = lax.fori_loop(0, NEIGH, scan_entry, count_ref[row], unroll=True)


def scan_lists(here, slots, near, live, n_row):
    smem = pl.BlockSpec(memory_space=pltpu.SMEM)
    return pl.pallas_call(
        scan_kernel,
        out_shape=(
            jax.ShapeDtypeStruct((n_row,), jnp.int32),
            jax.ShapeDtypeStruct((slots.shape[0] * NEIGH,), jnp.int32),
        ),
        in_specs=[smem] * 4,
        out_specs=(smem, smem),
    )(here, slots, near, live)


def grads_kernel(offsets, first, row_ref, count_ref, entry_ref, key_ref, value_ref, *refs):
    n_load = len(offsets)
    loads, refs = refs[:n_load], refs[n_load:]
    if not first:
        dk_old, dv_old = refs[:2]
        refs = refs[2:]
    dqs, refs = refs[:n_load], refs[n_load:]
    dk_acc, dv_acc, dq_acc, key_m, value_m, key_t = refs
    per_row = key_ref.shape[0]
    pairs = key_ref.shape[2] // PAIR
    room = NEIGH * per_row
    if first:
        dk_acc[...] = jnp.zeros_like(dk_acc)
        dv_acc[...] = jnp.zeros_like(dv_acc)
    else:
        dk_acc[...] = dk_old[...]
        dv_acc[...] = dv_old[...]

    low = lax.broadcasted_iota(jnp.int32, (BLOCK, PAIR), 1) < HEAD
    for c in range(pairs):
        lanes = slice(c * PAIR, (c + 1) * PAIR)

        @pl.loop(0, per_row)
        def _(t):
            key = key_ref[t, :, lanes].astype(jnp.float32) * SCALE
            value = value_ref[t, :, lanes].astype(jnp.float32)
            for h in range(2):
                mask = low if h == 0 else ~low
                part = slice(h * BLOCK, (h + 1) * BLOCK)
                masked = jnp.where(mask, key, 0.0)
                key_m[c, t, part] = masked.astype(jnp.bfloat16)
                value_m[c, t, part] = jnp.where(mask, value, 0.0).astype(jnp.bfloat16)
                key_t[c, t, :, part] = masked.T.astype(jnp.bfloat16)

    for i, (load_ref, dq_ref, offset) in enumerate(zip(loads, dqs, offsets)):
        source_row = row_ref[i]
        held = load_ref.shape[0]
        dq_acc[0:held] = jnp.zeros((held,) + dq_acc.shape[1:], jnp.float32)

        def add_entry(s, t, load_ref=load_ref):
            for c in range(pairs):
                lanes = slice(c * PAIR, (c + 1) * PAIR)
                query = load_ref[s, 0:BLOCK, lanes]
                grad = load_ref[s, BLOCK:2 * BLOCK, lanes]
                stats = load_ref[s, 2 * BLOCK:2 * BLOCK + STATS].astype(jnp.float32)
                score = nt(key_m[c, t], query)
                dprob = nt(value_m[c, t], grad)
                probs, dscores = [], []
                for h in range(2):
                    part = slice(h * BLOCK, (h + 1) * BLOCK)
                    i_h = 2 * c + h
                    norm = stats[i_h:i_h + 1]
                    delta = stats[2 * pairs + i_h:2 * pairs + i_h + 1]
                    prob = jnp.exp(score[part] - norm)
                    dscores.append((prob * (dprob[part] - delta)).astype(jnp.bfloat16))
                    probs.append(prob.astype(jnp.bfloat16))
                dv_acc[t, :, lanes] += jnp.where(low, nn(probs[0], grad), nn(probs[1], grad))
                dk_acc[t, :, lanes] += jnp.where(low, nn(dscores[0], query), nn(dscores[1], query))
                dq_acc[s, lanes] += nn(key_t[c, t], jnp.concatenate(dscores, axis=0))

        @pl.when(source_row >= 0)
        def _():
            @pl.loop(0, count_ref[source_row])
            def _(e):
                entry = entry_ref[source_row * room + e]
                s = entry // per_row - offset
                t = entry % per_row
                if held == per_row:
                    add_entry(s, t)
                else:
                    pl.when((s >= 0) & (s < held))(lambda: add_entry(s, t))

        dq_ref[...] = dq_acc[0:held].astype(jnp.bfloat16)


def stage_grads(rows, counts, entries, key, value, loads, offsets, carry):
    per_row, _, width = key.shape
    pairs = width // PAIR
    n_load = len(loads)
    smem = pl.BlockSpec(memory_space=pltpu.SMEM)
    vmem = pl.BlockSpec(memory_space=pltpu.VMEM)
    parts = tuple(
        jax.ShapeDtypeStruct((load.shape[0], width, BLOCK), jnp.bfloat16) for load in loads
    )
    total = jax.ShapeDtypeStruct(key.shape, jnp.float32)
    outs = pl.pallas_call(
        functools.partial(grads_kernel, offsets, not carry),
        out_shape=parts + (total, total),
        in_specs=[smem] * 3 + [vmem] * (2 + n_load + len(carry)),
        out_specs=(vmem,) * (n_load + 2),
        scratch_shapes=[
            pltpu.VMEM((per_row, width, BLOCK), jnp.float32),
            pltpu.VMEM((pairs, per_row, 2 * BLOCK, PAIR), jnp.bfloat16),
            pltpu.VMEM((pairs, per_row, 2 * BLOCK, PAIR), jnp.bfloat16),
            pltpu.VMEM((pairs, per_row, PAIR, 2 * BLOCK), jnp.bfloat16),
        ],
        compiler_params=pltpu.CompilerParams(vmem_limit_bytes=40 * 2**20),
        cost_estimate=pl.CostEstimate(
            flops=n_load * 3000000000, bytes_accessed=n_load * 2**21, transcendentals=0
        ),
    )(rows, counts, entries, key, value, *loads, *carry)
    return outs[:n_load], outs[n_load:]


def body(queries, keys, values, attended, grad_out, log_norms, block_slot, neighbours, live_count):
    n_row = lax.axis_size("row")
    here = lax.axis_index("row").astype(jnp.int32)
    n_z = n_row // 2
    z, y = here // 2, here % 2
    tokens, width = queries.shape
    per_row = tokens // BLOCK
    heads = log_norms.shape[1]

    def swap(x, low, high):
        pairs = [(2 * k + j, 2 * k + 1 - j) for k in range(low, high) for j in range(2)]
        return lax.ppermute(x, "row", pairs)

    def shift(x, by, low, high):
        pairs = [(2 * k + j, 2 * (k + by) + j) for k in range(low, high) for j in range(2)]
        return lax.ppermute(x, "row", pairs)

    delta = jnp.sum(
        (grad_out.astype(jnp.float32) * attended.astype(jnp.float32)).reshape(tokens, heads, HEAD),
        axis=2,
    ).astype(jnp.bfloat16)
    stats = jnp.concatenate([log_norms, delta], axis=1).reshape(per_row, BLOCK, 2 * heads)
    own = jnp.concatenate([
        queries.reshape(per_row, BLOCK, width),
        grad_out.reshape(per_row, BLOCK, width),
        jnp.transpose(stats, (0, 2, 1)),
        jnp.zeros((per_row, STATS - 2 * heads, width), jnp.bfloat16),
    ], axis=1)
    key = keys.reshape(per_row, BLOCK, width)
    value = values.reshape(per_row, BLOCK, width)

    last = n_z - 1
    half = per_row // 2
    edge = [(j, 2 + j) for j in range(2)] + [(2 * last + j, 2 * last - 2 + j) for j in range(2)]
    have = {("up", 0): own, ("y", 0): swap(own, 0, n_z)}
    ups, downs = own, own
    for k in range(1, n_z):
        ups = shift(ups, 1, k - 1, last)
        downs = shift(downs, -1, 1, n_z - k + 1)
        have[("up", k)], have[("down", k)] = ups, downs
        if k == 1:
            have[("y_up", 1)] = swap(ups, 2, n_z)
            have[("y_down", 1)] = swap(downs, 0, n_z - 2)
            have[("y_edge", 1)] = lax.ppermute(have[("y", 0)], "row", edge)
        elif k < last:
            have[("y_up", k)] = swap(ups, k, n_z)
            have[("y_down", k)] = swap(downs, 0, n_z - k)
        else:
            have[("y_up_a", k)] = swap(ups[:half], last, n_z)
            have[("y_down_a", k)] = swap(downs[:half], 0, 1)
            have[("y_up_b", k)] = shift(have[("y_up", k - 1)][half:], 1, last - 1, last)
            have[("y_down_b", k)] = shift(have[("y_down", k - 1)][half:], -1, 1, 2)

    counts, entries = scan_lists(
        here.reshape(1), block_slot, neighbours.reshape(-1), live_count, n_row
    )

    def named(kind, k):
        if kind == "y_edge":
            there = jnp.where(z == 1, 0, jnp.where(z == last - 1, last, -1))
        else:
            there = z + k if "down" in kind else z - k
            if (kind, k) == ("y_up", 1):
                there = jnp.where(there >= 1, there, -1)
            if (kind, k) == ("y_down", 1):
                there = jnp.where(there <= last - 1, there, -1)
        side = 1 - y if kind.startswith("y") else y
        return jnp.where((there >= 0) & (there < n_z), 2 * there + side, -1)

    stages = [[("up", 0)], [("y", 0), ("up", 1), ("down", 1)]]
    stages.append([("up", 2), ("down", 2), ("y_up", 1), ("y_down", 1), ("y_edge", 1)])
    for k in range(3, n_z):
        stages.append([("up", k), ("down", k), ("y_up", k - 1), ("y_down", k - 1)])
    stages.append([(kind, last) for kind in ("y_up_a", "y_down_a", "y_up_b", "y_down_b")])
    parts, carry = {}, ()
    for stage in stages:
        rows = jnp.stack([named(*name) for name in stage]).astype(jnp.int32)
        offsets = tuple(half if name[0].endswith("_b") else 0 for name in stage)
        dqs, carry = stage_grads(
            rows, counts, entries, key, value, [have[name] for name in stage], offsets, carry
        )
        parts.update(zip(stage, dqs))

    low = jnp.bfloat16

    def add(*terms):
        return sum(x.astype(jnp.float32) for x in terms)

    def add_half(x, part, lead):
        pads = ((0, per_row - half), (0, 0), (0, 0)) if lead else ((half, 0), (0, 0), (0, 0))
        return add(x, jnp.pad(part, pads)).astype(low)

    edge_back = lax.ppermute(parts[("y_edge", 1)], "row", [(j, i) for i, j in edge])
    up_b = shift(parts[("y_up_b", last)], -1, last, n_z)
    down_b = shift(parts[("y_down_b", last)], 1, 0, 1)
    up = add_half(parts[("up", last)], swap(parts[("y_up_a", last)], last, n_z), True)
    down = add_half(parts[("down", last)], swap(parts[("y_down_a", last)], 0, 1), True)
    for k in range(last - 1, 0, -1):
        up, down = shift(up, -1, k + 1, n_z), shift(down, 1, 0, n_z - k - 1)
        y_up, y_down = parts[("y_up", k)], parts[("y_down", k)]
        if k == last - 1:
            y_up, y_down = add_half(y_up, up_b, False), add_half(y_down, down_b, False)
        edged = k == 1
        y_up = swap(y_up, 2 if edged else k, n_z)
        y_down = swap(y_down, 0, n_z - 2 if edged else n_z - k)
        up = add(parts[("up", k)], y_up, up).astype(low)
        down = add(parts[("down", k)], y_down, down).astype(low)
    up, down = shift(up, -1, 1, n_z), shift(down, 1, 0, last)
    y_back = swap(add(parts[("y", 0)], edge_back).astype(low), 0, n_z)
    dq = add(parts[("up", 0)], y_back, up, down).astype(low)
    dk, dv = carry
    return (
        jnp.transpose(dq, (0, 2, 1)).reshape(tokens, width),
        (dk * SCALE).astype(low).reshape(tokens, width),
        dv.astype(low).reshape(tokens, width),
    )


def solution(mesh):
    tokens = P(("groups", "row"), "col")
    return jax.shard_map(
        body,
        mesh=mesh,
        in_specs=(tokens,) * 6 + (P("groups"), P("groups", None), P("groups")),
        out_specs=(tokens,) * 3,
        check_vma=False,
    )
```

```python
import functools

import jax
import jax.numpy as jnp
from jax import lax
from jax.experimental import pallas as pl
from jax.experimental.pallas import tpu as pltpu
from jax.sharding import PartitionSpec as P

BLOCK = 256
NEIGH = 8
SCALE = 0.125
HEAD = 64
PAIR = 2 * HEAD
STATS = 16


def nt(a, b):
    return lax.dot_general(a, b, (((1,), (1,)), ((), ())), preferred_element_type=jnp.float32)


def nn(a, b):
    return lax.dot_general(a, b, (((1,), (0,)), ((), ())), preferred_element_type=jnp.float32)


def scan_kernel(here_ref, slot_ref, near_ref, live_ref, count_ref, entry_ref):
    blocks = slot_ref.shape[0]
    n_row = count_ref.shape[0]
    per_row = blocks // n_row
    first = here_ref[0] * per_row
    room = NEIGH * per_row

    @pl.loop(0, n_row)
    def _(r):
        count_ref[r] = 0

    @pl.loop(0, blocks)
    def _(b):
        source = slot_ref[b]
        row = source // per_row
        live = live_ref[b]

        def scan_entry(j, count):
            target = slot_ref[near_ref[b * NEIGH + j]] - first
            mine = (target >= 0) & (target < per_row) & (j < live)

            @pl.when(mine)
            def _():
                entry_ref[row * room + count] = (source - row * per_row) * per_row + target

            return count + mine.astype(jnp.int32)

        count_ref[row] = lax.fori_loop(0, NEIGH, scan_entry, count_ref[row], unroll=True)


def scan_lists(here, slots, near, live, n_row):
    smem = pl.BlockSpec(memory_space=pltpu.SMEM)
    return pl.pallas_call(
        scan_kernel,
        out_shape=(
            jax.ShapeDtypeStruct((n_row,), jnp.int32),
            jax.ShapeDtypeStruct((slots.shape[0] * NEIGH,), jnp.int32),
        ),
        in_specs=[smem] * 4,
        out_specs=(smem, smem),
    )(here, slots, near, live)


def grads_kernel(offsets, first, row_ref, count_ref, entry_ref, key_ref, value_ref, *refs):
    n_load = len(offsets)
    loads, refs = refs[:n_load], refs[n_load:]
    if not first:
        dk_old, dv_old = refs[:2]
        refs = refs[2:]
    dqs, refs = refs[:n_load], refs[n_load:]
    dk_acc, dv_acc, dq_acc, key_m, value_m, key_t = refs
    per_row = key_ref.shape[0]
    pairs = key_ref.shape[2] // PAIR
    room = NEIGH * per_row
    if first:
        dk_acc[...] = jnp.zeros_like(dk_acc)
        dv_acc[...] = jnp.zeros_like(dv_acc)
    else:
        dk_acc[...] = dk_old[...]
        dv_acc[...] = dv_old[...]

    low = lax.broadcasted_iota(jnp.int32, (BLOCK, PAIR), 1) < HEAD
    for c in range(pairs):
        lanes = slice(c * PAIR, (c + 1) * PAIR)

        @pl.loop(0, per_row)
        def _(t):
            key = key_ref[t, :, lanes].astype(jnp.float32) * SCALE
            value = value_ref[t, :, lanes].astype(jnp.float32)
            for h in range(2):
                mask = low if h == 0 else ~low
                part = slice(h * BLOCK, (h + 1) * BLOCK)
                masked = jnp.where(mask, key, 0.0)
                key_m[c, t, part] = masked.astype(jnp.bfloat16)
                value_m[c, t, part] = jnp.where(mask, value, 0.0).astype(jnp.bfloat16)
                key_t[c, t, :, part] = masked.T.astype(jnp.bfloat16)

    for i, (load_ref, dq_ref, offset) in enumerate(zip(loads, dqs, offsets)):
        source_row = row_ref[i]
        held = load_ref.shape[0]
        dq_acc[0:held] = jnp.zeros((held,) + dq_acc.shape[1:], jnp.float32)

        def add_entry(s, t, load_ref=load_ref):
            for c in range(pairs):
                lanes = slice(c * PAIR, (c + 1) * PAIR)
                query = load_ref[s, 0:BLOCK, lanes]
                grad = load_ref[s, BLOCK:2 * BLOCK, lanes]
                stats = load_ref[s, 2 * BLOCK:2 * BLOCK + STATS].astype(jnp.float32)
                score = nt(key_m[c, t], query)
                dprob = nt(value_m[c, t], grad)
                probs, dscores = [], []
                for h in range(2):
                    part = slice(h * BLOCK, (h + 1) * BLOCK)
                    i_h = 2 * c + h
                    norm = stats[i_h:i_h + 1]
                    delta = stats[2 * pairs + i_h:2 * pairs + i_h + 1]
                    prob = jnp.exp(score[part] - norm)
                    dscores.append((prob * (dprob[part] - delta)).astype(jnp.bfloat16))
                    probs.append(prob.astype(jnp.bfloat16))
                dv_acc[t, :, lanes] += jnp.where(low, nn(probs[0], grad), nn(probs[1], grad))
                dk_acc[t, :, lanes] += jnp.where(low, nn(dscores[0], query), nn(dscores[1], query))
                dq_acc[s, lanes] += nn(key_t[c, t], jnp.concatenate(dscores, axis=0))

        @pl.when(source_row >= 0)
        def _():
            @pl.loop(0, count_ref[source_row])
            def _(e):
                entry = entry_ref[source_row * room + e]
                s = entry // per_row - offset
                t = entry % per_row
                if held == per_row:
                    add_entry(s, t)
                else:
                    pl.when((s >= 0) & (s < held))(lambda: add_entry(s, t))

        dq_ref[...] = dq_acc[0:held].astype(jnp.bfloat16)


def stage_grads(rows, counts, entries, key, value, loads, offsets, carry):
    per_row, _, width = key.shape
    pairs = width // PAIR
    n_load = len(loads)
    smem = pl.BlockSpec(memory_space=pltpu.SMEM)
    vmem = pl.BlockSpec(memory_space=pltpu.VMEM)
    parts = tuple(
        jax.ShapeDtypeStruct((load.shape[0], width, BLOCK), jnp.bfloat16) for load in loads
    )
    total = jax.ShapeDtypeStruct(key.shape, jnp.float32)
    outs = pl.pallas_call(
        functools.partial(grads_kernel, offsets, not carry),
        out_shape=parts + (total, total),
        in_specs=[smem] * 3 + [vmem] * (2 + n_load + len(carry)),
        out_specs=(vmem,) * (n_load + 2),
        scratch_shapes=[
            pltpu.VMEM((per_row, width, BLOCK), jnp.float32),
            pltpu.VMEM((pairs, per_row, 2 * BLOCK, PAIR), jnp.bfloat16),
            pltpu.VMEM((pairs, per_row, 2 * BLOCK, PAIR), jnp.bfloat16),
            pltpu.VMEM((pairs, per_row, PAIR, 2 * BLOCK), jnp.bfloat16),
        ],
        compiler_params=pltpu.CompilerParams(vmem_limit_bytes=58 * 2**20),
        cost_estimate=pl.CostEstimate(
            flops=n_load * 3000000000, bytes_accessed=n_load * 2**21, transcendentals=0
        ),
    )(rows, counts, entries, key, value, *loads, *carry)
    return outs[:n_load], outs[n_load:]


def body(queries, keys, values, attended, grad_out, log_norms, block_slot, neighbours, live_count):
    n_row = lax.axis_size("row")
    here = lax.axis_index("row").astype(jnp.int32)
    n_z = n_row // 2
    z, y = here // 2, here % 2
    tokens, width = queries.shape
    per_row = tokens // BLOCK
    heads = log_norms.shape[1]

    def swap(x, low, high):
        pairs = [(2 * k + j, 2 * k + 1 - j) for k in range(low, high) for j in range(2)]
        return lax.ppermute(x, "row", pairs)

    def shift(x, by, low, high):
        pairs = [(2 * k + j, 2 * (k + by) + j) for k in range(low, high) for j in range(2)]
        return lax.ppermute(x, "row", pairs)

    delta = jnp.sum(
        (grad_out.astype(jnp.float32) * attended.astype(jnp.float32)).reshape(tokens, heads, HEAD),
        axis=2,
    ).astype(jnp.bfloat16)
    stats = jnp.concatenate([log_norms, delta], axis=1).reshape(per_row, BLOCK, 2 * heads)
    own = jnp.concatenate([
        queries.reshape(per_row, BLOCK, width),
        grad_out.reshape(per_row, BLOCK, width),
        jnp.transpose(stats, (0, 2, 1)),
        jnp.zeros((per_row, STATS - 2 * heads, width), jnp.bfloat16),
    ], axis=1)
    key = keys.reshape(per_row, BLOCK, width)
    value = values.reshape(per_row, BLOCK, width)

    last = n_z - 1
    half = per_row // 2
    edge = [(j, 2 + j) for j in range(2)] + [(2 * last + j, 2 * last - 2 + j) for j in range(2)]
    counts, entries = scan_lists(
        here.reshape(1), block_slot, neighbours.reshape(-1), live_count, n_row
    )

    have = {("up", 0): own, ("y", 0): swap(own, 0, n_z)}
    (own_part,), carry = stage_grads(
        here.reshape(1), counts, entries, key, value, [own], (0,), ()
    )
    ups, downs = own, own
    for k in range(1, n_z):
        ups = shift(ups, 1, k - 1, last)
        downs = shift(downs, -1, 1, n_z - k + 1)
        if k == 1:
            ups, downs, carry, own_part = lax.optimization_barrier((ups, downs, carry, own_part))
        have[("up", k)], have[("down", k)] = ups, downs
        if k == 1:
            have[("y_up", 1)] = swap(ups, 2, n_z)
            have[("y_down", 1)] = swap(downs, 0, n_z - 2)
            have[("y_edge", 1)] = lax.ppermute(have[("y", 0)], "row", edge)
        elif k < last:
            have[("y_up", k)] = swap(ups, k, n_z)
            have[("y_down", k)] = swap(downs, 0, n_z - k)
        else:
            have[("y_up_a", k)] = swap(ups[:half], last, n_z)
            have[("y_down_a", k)] = swap(downs[:half], 0, 1)
            have[("y_up_b", k)] = shift(have[("y_up", k - 1)][half:], 1, last - 1, last)
            have[("y_down_b", k)] = shift(have[("y_down", k - 1)][half:], -1, 1, 2)

    def named(kind, k):
        if kind == "y_edge":
            there = jnp.where(z == 1, 0, jnp.where(z == last - 1, last, -1))
        else:
            there = z + k if "down" in kind else z - k
            if (kind, k) == ("y_up", 1):
                there = jnp.where(there >= 1, there, -1)
            if (kind, k) == ("y_down", 1):
                there = jnp.where(there <= last - 1, there, -1)
        side = 1 - y if kind.startswith("y") else y
        return jnp.where((there >= 0) & (there < n_z), 2 * there + side, -1)

    stages = [[("y", 0), ("up", 1), ("down", 1)]]
    stages.append([("up", 2), ("down", 2), ("y_up", 1), ("y_down", 1), ("y_edge", 1)])
    for k in range(3, n_z):
        stages.append([("up", k), ("down", k), ("y_up", k - 1), ("y_down", k - 1)])
    stages.append([(kind, last) for kind in ("y_up_a", "y_down_a", "y_up_b", "y_down_b")])
    parts = {("up", 0): own_part}
    for stage in stages:
        rows = jnp.stack([named(*name) for name in stage]).astype(jnp.int32)
        offsets = tuple(half if name[0].endswith("_b") else 0 for name in stage)
        dqs, carry = stage_grads(
            rows, counts, entries, key, value, [have[name] for name in stage], offsets, carry
        )
        parts.update(zip(stage, dqs))

    low = jnp.bfloat16

    def add(*terms):
        return sum(x.astype(jnp.float32) for x in terms)

    def add_half(x, part, lead):
        pads = ((0, per_row - half), (0, 0), (0, 0)) if lead else ((half, 0), (0, 0), (0, 0))
        return add(x, jnp.pad(part, pads)).astype(low)

    edge_back = lax.ppermute(parts[("y_edge", 1)], "row", [(j, i) for i, j in edge])
    up_b = shift(parts[("y_up_b", last)], -1, last, n_z)
    down_b = shift(parts[("y_down_b", last)], 1, 0, 1)
    up = add_half(parts[("up", last)], swap(parts[("y_up_a", last)], last, n_z), True)
    down = add_half(parts[("down", last)], swap(parts[("y_down_a", last)], 0, 1), True)
    for k in range(last - 1, 0, -1):
        up, down = shift(up, -1, k + 1, n_z), shift(down, 1, 0, n_z - k - 1)
        y_up, y_down = parts[("y_up", k)], parts[("y_down", k)]
        if k == last - 1:
            y_up, y_down = add_half(y_up, up_b, False), add_half(y_down, down_b, False)
        edged = k == 1
        y_up = swap(y_up, 2 if edged else k, n_z)
        y_down = swap(y_down, 0, n_z - 2 if edged else n_z - k)
        up = add(parts[("up", k)], y_up, up).astype(low)
        down = add(parts[("down", k)], y_down, down).astype(low)
    up, down = shift(up, -1, 1, n_z), shift(down, 1, 0, last)
    y_back = swap(add(parts[("y", 0)], edge_back).astype(low), 0, n_z)
    dq = add(parts[("up", 0)], y_back, up, down).astype(low)
    dk, dv = carry
    return (
        jnp.transpose(dq, (0, 2, 1)).reshape(tokens, width),
        (dk * SCALE).astype(low).reshape(tokens, width),
        dv.astype(low).reshape(tokens, width),
    )


def solution(mesh):
    tokens = P(("groups", "row"), "col")
    return jax.shard_map(
        body,
        mesh=mesh,
        in_specs=(tokens,) * 6 + (P("groups"), P("groups", None), P("groups")),
        out_specs=(tokens,) * 3,
        check_vma=False,
    )
```

```python
import functools

import jax
import jax.numpy as jnp
from jax import lax
from jax.experimental import pallas as pl
from jax.experimental.pallas import tpu as pltpu
from jax.sharding import PartitionSpec as P

BLOCK = 256
NEIGH = 8
SCALE = 0.125
HEAD = 64
PAIR = 2 * HEAD
STATS = 16


def nt(a, b):
    return lax.dot_general(a, b, (((1,), (1,)), ((), ())), preferred_element_type=jnp.float32)


def nn(a, b):
    return lax.dot_general(a, b, (((1,), (0,)), ((), ())), preferred_element_type=jnp.float32)


def scan_kernel(here_ref, slot_ref, near_ref, live_ref, count_ref, entry_ref):
    blocks = slot_ref.shape[0]
    n_row = count_ref.shape[0]
    per_row = blocks // n_row
    first = here_ref[0] * per_row
    room = NEIGH * per_row

    @pl.loop(0, n_row)
    def _(r):
        count_ref[r] = 0

    @pl.loop(0, blocks)
    def _(b):
        source = slot_ref[b]
        row = source // per_row
        live = live_ref[b]

        def scan_entry(j, count):
            target = slot_ref[near_ref[b * NEIGH + j]] - first
            mine = (target >= 0) & (target < per_row) & (j < live)

            @pl.when(mine)
            def _():
                entry_ref[row * room + count] = (source - row * per_row) * per_row + target

            return count + mine.astype(jnp.int32)

        count_ref[row] = lax.fori_loop(0, NEIGH, scan_entry, count_ref[row], unroll=True)


def scan_lists(here, slots, near, live, n_row):
    smem = pl.BlockSpec(memory_space=pltpu.SMEM)
    return pl.pallas_call(
        scan_kernel,
        out_shape=(
            jax.ShapeDtypeStruct((n_row,), jnp.int32),
            jax.ShapeDtypeStruct((slots.shape[0] * NEIGH,), jnp.int32),
        ),
        in_specs=[smem] * 4,
        out_specs=(smem, smem),
    )(here, slots, near, live)


def grads_kernel(offsets, first, row_ref, count_ref, entry_ref, key_ref, value_ref, *refs):
    n_load = len(offsets)
    loads, refs = refs[:n_load], refs[n_load:]
    if not first:
        dk_old, dv_old = refs[:2]
        refs = refs[2:]
    dqs, refs = refs[:n_load], refs[n_load:]
    dk_acc, dv_acc, dq_acc, key_m, value_m, key_t = refs
    per_row = key_ref.shape[0]
    pairs = key_ref.shape[2] // PAIR
    room = NEIGH * per_row
    if first:
        dk_acc[...] = jnp.zeros_like(dk_acc)
        dv_acc[...] = jnp.zeros_like(dv_acc)
    else:
        dk_acc[...] = dk_old[...]
        dv_acc[...] = dv_old[...]

    low = lax.broadcasted_iota(jnp.int32, (BLOCK, PAIR), 1) < HEAD
    for c in range(pairs):
        lanes = slice(c * PAIR, (c + 1) * PAIR)

        @pl.loop(0, per_row)
        def _(t):
            key = key_ref[t, :, lanes].astype(jnp.float32) * SCALE
            value = value_ref[t, :, lanes].astype(jnp.float32)
            for h in range(2):
                mask = low if h == 0 else ~low
                part = slice(h * BLOCK, (h + 1) * BLOCK)
                masked = jnp.where(mask, key, 0.0)
                key_m[c, t, part] = masked.astype(jnp.bfloat16)
                value_m[c, t, part] = jnp.where(mask, value, 0.0).astype(jnp.bfloat16)
                key_t[c, t, :, part] = masked.T.astype(jnp.bfloat16)

    for i, (load_ref, dq_ref, offset) in enumerate(zip(loads, dqs, offsets)):
        source_row = row_ref[i]
        held = load_ref.shape[0]
        dq_acc[0:held] = jnp.zeros((held,) + dq_acc.shape[1:], jnp.float32)

        def add_entry(s, t, load_ref=load_ref):
            for c in range(pairs):
                lanes = slice(c * PAIR, (c + 1) * PAIR)
                query = load_ref[s, 0:BLOCK, lanes]
                grad = load_ref[s, BLOCK:2 * BLOCK, lanes]
                stats = load_ref[s, 2 * BLOCK:2 * BLOCK + STATS].astype(jnp.float32)
                score = nt(key_m[c, t], query)
                dprob = nt(value_m[c, t], grad)
                probs, dscores = [], []
                for h in range(2):
                    part = slice(h * BLOCK, (h + 1) * BLOCK)
                    i_h = 2 * c + h
                    norm = stats[i_h:i_h + 1]
                    delta = stats[2 * pairs + i_h:2 * pairs + i_h + 1]
                    prob = jnp.exp(score[part] - norm)
                    dscores.append((prob * (dprob[part] - delta)).astype(jnp.bfloat16))
                    probs.append(prob.astype(jnp.bfloat16))
                dv_acc[t, :, lanes] += jnp.where(low, nn(probs[0], grad), nn(probs[1], grad))
                dk_acc[t, :, lanes] += jnp.where(low, nn(dscores[0], query), nn(dscores[1], query))
                dq_acc[s, lanes] += nn(key_t[c, t], jnp.concatenate(dscores, axis=0))

        @pl.when(source_row >= 0)
        def _():
            @pl.loop(0, count_ref[source_row])
            def _(e):
                entry = entry_ref[source_row * room + e]
                s = entry // per_row - offset
                t = entry % per_row
                if held == per_row:
                    add_entry(s, t)
                else:
                    pl.when((s >= 0) & (s < held))(lambda: add_entry(s, t))

        dq_ref[...] = dq_acc[0:held].astype(jnp.bfloat16)


def stage_grads(rows, counts, entries, key, value, loads, offsets, carry):
    per_row, _, width = key.shape
    pairs = width // PAIR
    n_load = len(loads)
    smem = pl.BlockSpec(memory_space=pltpu.SMEM)
    vmem = pl.BlockSpec(memory_space=pltpu.VMEM)
    parts = tuple(
        jax.ShapeDtypeStruct((load.shape[0], width, BLOCK), jnp.bfloat16) for load in loads
    )
    total = jax.ShapeDtypeStruct(key.shape, jnp.float32)
    outs = pl.pallas_call(
        functools.partial(grads_kernel, offsets, not carry),
        out_shape=parts + (total, total),
        in_specs=[smem] * 3 + [vmem] * (2 + n_load + len(carry)),
        out_specs=(vmem,) * (n_load + 2),
        scratch_shapes=[
            pltpu.VMEM((per_row, width, BLOCK), jnp.float32),
            pltpu.VMEM((pairs, per_row, 2 * BLOCK, PAIR), jnp.bfloat16),
            pltpu.VMEM((pairs, per_row, 2 * BLOCK, PAIR), jnp.bfloat16),
            pltpu.VMEM((pairs, per_row, PAIR, 2 * BLOCK), jnp.bfloat16),
        ],
        compiler_params=pltpu.CompilerParams(vmem_limit_bytes=40 * 2**20),
        cost_estimate=pl.CostEstimate(
            flops=n_load * 3000000000, bytes_accessed=n_load * 2**21, transcendentals=0
        ),
    )(rows, counts, entries, key, value, *loads, *carry)
    return outs[:n_load], outs[n_load:]


def body(queries, keys, values, attended, grad_out, log_norms, block_slot, neighbours, live_count):
    n_row = lax.axis_size("row")
    here = lax.axis_index("row").astype(jnp.int32)
    n_z = n_row // 2
    z, y = here // 2, here % 2
    tokens, width = queries.shape
    per_row = tokens // BLOCK
    heads = log_norms.shape[1]

    def swap(x, low, high):
        pairs = [(2 * k + j, 2 * k + 1 - j) for k in range(low, high) for j in range(2)]
        return lax.ppermute(x, "row", pairs)

    def shift(x, by, low, high):
        pairs = [(2 * k + j, 2 * (k + by) + j) for k in range(low, high) for j in range(2)]
        return lax.ppermute(x, "row", pairs)

    delta = jnp.sum(
        (grad_out.astype(jnp.float32) * attended.astype(jnp.float32)).reshape(tokens, heads, HEAD),
        axis=2,
    ).astype(jnp.bfloat16)
    stats = jnp.concatenate([log_norms, delta], axis=1).reshape(per_row, BLOCK, 2 * heads)
    own = jnp.concatenate([
        queries.reshape(per_row, BLOCK, width),
        grad_out.reshape(per_row, BLOCK, width),
        jnp.transpose(stats, (0, 2, 1)),
        jnp.zeros((per_row, STATS - 2 * heads, width), jnp.bfloat16),
    ], axis=1)
    key = keys.reshape(per_row, BLOCK, width)
    value = values.reshape(per_row, BLOCK, width)

    last = n_z - 1
    half = per_row // 2
    edge = [(j, 2 + j) for j in range(2)] + [(2 * last + j, 2 * last - 2 + j) for j in range(2)]
    counts, entries = scan_lists(
        here.reshape(1), block_slot, neighbours.reshape(-1), live_count, n_row
    )

    have = {("up", 0): own, ("y", 0): swap(own, 0, n_z)}
    (own_part,), carry = stage_grads(
        here.reshape(1), counts, entries, key, value, [own], (0,), ()
    )
    ups, downs = own, own
    for k in range(1, n_z):
        ups = shift(ups, 1, k - 1, last)
        downs = shift(downs, -1, 1, n_z - k + 1)
        if k == 1:
            ups, carry, own_part = lax.optimization_barrier((ups, carry, own_part))
        have[("up", k)], have[("down", k)] = ups, downs
        if k == 1:
            have[("y_up", 1)] = swap(ups, 2, n_z)
            have[("y_down", 1)] = swap(downs, 0, n_z - 2)
            have[("y_edge", 1)] = lax.ppermute(have[("y", 0)], "row", edge)
        elif k < last:
            have[("y_up", k)] = swap(ups, k, n_z)
            have[("y_down", k)] = swap(downs, 0, n_z - k)
        else:
            have[("y_up_a", k)] = swap(ups[:half], last, n_z)
            have[("y_down_a", k)] = swap(downs[:half], 0, 1)
            have[("y_up_b", k)] = shift(have[("y_up", k - 1)][half:], 1, last - 1, last)
            have[("y_down_b", k)] = shift(have[("y_down", k - 1)][half:], -1, 1, 2)

    def named(kind, k):
        if kind == "y_edge":
            there = jnp.where(z == 1, 0, jnp.where(z == last - 1, last, -1))
        else:
            there = z + k if "down" in kind else z - k
            if (kind, k) == ("y_up", 1):
                there = jnp.where(there >= 1, there, -1)
            if (kind, k) == ("y_down", 1):
                there = jnp.where(there <= last - 1, there, -1)
        side = 1 - y if kind.startswith("y") else y
        return jnp.where((there >= 0) & (there < n_z), 2 * there + side, -1)

    stages = [[("y", 0), ("up", 1), ("down", 1)]]
    stages.append([("up", 2), ("down", 2), ("y_up", 1), ("y_down", 1), ("y_edge", 1)])
    for k in range(3, n_z):
        stages.append([("up", k), ("down", k), ("y_up", k - 1), ("y_down", k - 1)])
    stages.append([(kind, last) for kind in ("y_up_a", "y_down_a", "y_up_b", "y_down_b")])
    parts = {("up", 0): own_part}
    for stage in stages:
        rows = jnp.stack([named(*name) for name in stage]).astype(jnp.int32)
        offsets = tuple(half if name[0].endswith("_b") else 0 for name in stage)
        dqs, carry = stage_grads(
            rows, counts, entries, key, value, [have[name] for name in stage], offsets, carry
        )
        parts.update(zip(stage, dqs))

    low = jnp.bfloat16

    def add(*terms):
        return sum(x.astype(jnp.float32) for x in terms)

    def add_half(x, part, lead):
        pads = ((0, per_row - half), (0, 0), (0, 0)) if lead else ((half, 0), (0, 0), (0, 0))
        return add(x, jnp.pad(part, pads)).astype(low)

    edge_back = lax.ppermute(parts[("y_edge", 1)], "row", [(j, i) for i, j in edge])
    up_b = shift(parts[("y_up_b", last)], -1, last, n_z)
    down_b = shift(parts[("y_down_b", last)], 1, 0, 1)
    up = add_half(parts[("up", last)], swap(parts[("y_up_a", last)], last, n_z), True)
    down = add_half(parts[("down", last)], swap(parts[("y_down_a", last)], 0, 1), True)
    for k in range(last - 1, 0, -1):
        up, down = shift(up, -1, k + 1, n_z), shift(down, 1, 0, n_z - k - 1)
        y_up, y_down = parts[("y_up", k)], parts[("y_down", k)]
        if k == last - 1:
            y_up, y_down = add_half(y_up, up_b, False), add_half(y_down, down_b, False)
        edged = k == 1
        y_up = swap(y_up, 2 if edged else k, n_z)
        y_down = swap(y_down, 0, n_z - 2 if edged else n_z - k)
        up = add(parts[("up", k)], y_up, up).astype(low)
        down = add(parts[("down", k)], y_down, down).astype(low)
    up, down = shift(up, -1, 1, n_z), shift(down, 1, 0, last)
    y_back = swap(add(parts[("y", 0)], edge_back).astype(low), 0, n_z)
    dq = add(parts[("up", 0)], y_back, up, down).astype(low)
    dk, dv = carry
    return (
        jnp.transpose(dq, (0, 2, 1)).reshape(tokens, width),
        (dk * SCALE).astype(low).reshape(tokens, width),
        dv.astype(low).reshape(tokens, width),
    )


def solution(mesh):
    tokens = P(("groups", "row"), "col")
    return jax.shard_map(
        body,
        mesh=mesh,
        in_specs=(tokens,) * 6 + (P("groups"), P("groups", None), P("groups")),
        out_specs=(tokens,) * 3,
        check_vma=False,
    )
```
